256 devices in a mesh: dp: 8 (over y, z_hi), owner: 32 (over x, z_lo, core).
Axes of the slice: x: 4, y: 4, z: 8 (z_hi: 2, z_lo: 4; z = z_hi * 4 + z_lo), core: 2. Of those that a mesh axis runs over, the one named last changes fastest.
Arguments:
- grad_parts: bfloat16 [8, 128, 512, 512], P('dp', None, 'owner'), may hold values from -2.5 to 2.5
- stats: float32 [256, 512, 512], P(('dp', 'owner')), may hold values from -10 to 12, as said below
- roots: bfloat16 [256, 512, 512], P(('dp', 'owner')), may hold values from -0.25 to 0.25
- refresh: int32 [128], P('dp'), may hold values 0 or 1
Outputs:
- new_stats: float32 [256, 512, 512], P(('dp', 'owner'))
- new_roots: bfloat16 [256, 512, 512], P(('dp', 'owner'))
- update: bfloat16 [128, 512, 512], P('dp', 'owner')
The draws below stay inside these ranges and needn't reach their ends.
Inputs may be any that keep to these rules, and one draw needn't show every extreme that they name: Every stats matrix is symmetric positive definite.
All inputs are finite; a program needn't handle non-finite values. No bound on the sum of `refresh` on one device may be relied on, other than what follows from the above.
Results may differ from the reference program's by a relative error of at most 0.015.
Values may be sent and summed in bfloat16 or wider, within the bound.
A program may use at most 64 MiB of HBM per device.

```python
import jax
import jax.numpy as jnp
from jax import lax

BS = 512
ITERS = 5
BLOCKS = 128
N_DP = 8


def draw_stats(key, part):
    first = jax.random.fold_in(key, 11)
    second = jax.random.fold_in(key, 12)
    third = jax.random.fold_in(key, 13)
    factors = jnp.clip(jax.random.normal(first, (2 * BLOCKS, BS, BS // 4), jnp.float32), -3.0, 3.0)
    scales = jnp.exp(jax.random.uniform(second, (2 * BLOCKS, BS), jnp.float32, -1.1512925, 0.0))
    base = jnp.einsum('mik,mjk->mij', factors, factors) / (BS // 4)
    diagonal = jax.random.uniform(third, (2 * BLOCKS, BS), jnp.float32, 1.0, 2.0) * scales * scales
    eye = jnp.eye(BS, dtype=jnp.float32)
    return scales[:, :, None] * scales[:, None, :] * base + diagonal[:, :, None] * eye


def plant(entries, stream_key, least, top_value):
    shape = entries.shape
    index_at = [jax.random.randint(jax.random.fold_in(stream_key, axis), (), 0, shape[axis]) for axis in range(len(shape))]
    entries = entries.at[tuple(index_at)].set(least)
    longest = shape.index(max(shape))
    index_at[longest] = (index_at[longest] + 1) % shape[longest]
    return entries.at[tuple(index_at)].set(top_value)


def raised(drawn, stream_key, source, target, shards_of, factor):
    def block_of(dim):
        return (jnp.arange(drawn.shape[dim]) // (drawn.shape[dim] // shards_of)).reshape((-1,) + (1,) * (drawn.ndim - 1 - dim))

    first = jax.random.permutation(stream_key, shards_of)[block_of(target)]
    second = (block_of(target) + shards_of // 2) % shards_of
    return jnp.where((block_of(source) == first) | (block_of(source) == second), factor * drawn, drawn)


def levels(stream_key, shape, split, least, high):
    level = 1.0
    for position, shards_of in split:
        steps = jax.random.uniform(jax.random.fold_in(jax.random.fold_in(stream_key, 6), position), (shards_of,), jnp.float32, least / len(split), high / len(split))
        level = level * jnp.repeat(jnp.exp(steps), shape[position] // shards_of).reshape((-1,) + (1,) * (len(shape) - 1 - position))
    return level


def normal_values(key, shape, width, reach, cuts=(), held_as=jnp.bfloat16):
    values = width * jax.random.normal(key, shape, jnp.float32)
    if cuts:
        values = values * levels(key, shape, cuts, -0.22, 0.18)
    return jnp.clip(values, -reach, reach).astype(held_as)


def bell_draw_with(own_key, extent, deviation, bound, cuts, heavy, kind=jnp.bfloat16):
    entries = deviation * jax.random.normal(own_key, extent, jnp.float32)
    if cuts:
        entries = entries * levels(own_key, extent, cuts, -0.22, 0.18)
    return jnp.clip(raised(entries, jax.random.fold_in(own_key, 3), *heavy), -bound, bound).astype(kind)


def setup_inputs(seed: int = 0) -> dict:
    seeds = jax.random.split(jax.random.key(seed), 5)
    grad_parts = bell_draw_with(seeds[0], (N_DP, BLOCKS, BS, BS), 0.35, 2.5, ((0, 8), (2, 32)), (0, 1, 8, 2.0))
    stats = draw_stats(jax.random.fold_in(seeds[4], 71), 0)
    roots = normal_values(seeds[2], (2 * BLOCKS, BS, BS), BS ** -0.5, 0.25, ((0, 256),))
    refresh = plant((jax.random.randint(seeds[3], (BLOCKS,), 0, 2) < 1).astype(jnp.int32), jax.random.fold_in(seeds[3], 1), 0, 1)
    return dict(grad_parts=grad_parts, stats=stats, roots=roots, refresh=refresh)


BETA = 0.8

def inverse_root(matrix):
    size = matrix.shape[0]
    eye = jnp.eye(size, dtype=jnp.float32)
    scale = jnp.sqrt(jnp.sum(matrix * matrix) + 1e-06)
    current = matrix / scale
    result = eye * scale ** (-0.25)
    for step in range(ITERS):
        factor = (5.0 * eye - current) / 4.0
        result = jnp.dot(result, factor, precision=lax.Precision.HIGHEST)
        if step + 1 < ITERS:
            square = jnp.dot(factor, factor, precision=lax.Precision.HIGHEST)
            fourth = jnp.dot(square, square, precision=lax.Precision.HIGHEST)
            current = jnp.dot(fourth, current, precision=lax.Precision.HIGHEST)
    return result

def reference(grad_parts, stats, roots, refresh):
    grad = lax.optimization_barrier(jnp.sum(grad_parts.astype(jnp.float32), axis=0)).astype(jnp.bfloat16)
    pair_stats = stats.reshape(BLOCKS, 2, BS, BS)
    pair_roots = roots.reshape(BLOCKS, 2, BS, BS)

    def per_block(items):
        block, old_stats, old_roots, flag = items
        wide = block.astype(jnp.float32)
        left = jnp.dot(wide, wide.T, precision=lax.Precision.HIGHEST) / BS
        right = jnp.dot(wide.T, wide, precision=lax.Precision.HIGHEST) / BS
        fresh = BETA * old_stats + (1.0 - BETA) * jnp.stack([left, right])
        solved = jnp.stack([inverse_root(fresh[0]), inverse_root(fresh[1])])
        chosen = jnp.where(flag == 1, solved.astype(jnp.bfloat16), old_roots)
        product = jnp.dot(old_roots[0], block, preferred_element_type=jnp.float32).astype(jnp.bfloat16)
        result = jnp.dot(product, old_roots[1], preferred_element_type=jnp.float32).astype(jnp.bfloat16)
        return (fresh, chosen, result)
    fresh, chosen, update = lax.map(per_block, (grad, pair_stats, pair_roots, refresh))
    return (fresh.reshape(2 * BLOCKS, BS, BS), chosen.reshape(2 * BLOCKS, BS, BS), update)
```

```python
import functools

import jax
import jax.numpy as jnp
from jax import lax
from jax.experimental import pallas as pl
from jax.experimental.pallas import tpu as pltpu
from jax.sharding import PartitionSpec as P

MESH = pl.DeviceIdType.MESH
BF = jnp.bfloat16
F32 = jnp.float32
BS = 512
ITERS = 5
BETA = 0.8
NY, NZH, NX, NZL, NC = 4, 2, 4, 4, 2
ROWS = 16
TILE = 128
ORDER = (2, 1, 3, 0)


def kernel(
    gp, stats, roots, refresh,
    new_stats, new_roots, update,
    own, side_p, side_m, r1p, r1m, r2ap, r2am, r2bp, r2bm, zrecv, gfull, st, rt, other,
    m32, mb, x32, xb, n32, nb, wb, prod, upd, root_out,
    load_sem, y_send, y_recv, z_send, z_recv, c_send, c_recv, u_send, u_recv, out_sem,
):
    dp = lax.axis_index("dp")
    owner = lax.axis_index("owner")
    y, zh = dp // NZH, dp % NZH
    x, zl, c = owner // (NZL * NC), (owner // NC) % NZL, owner % NC

    def dev(yy, zz, xx, ll, cc):
        return (yy * NZH + zz, (xx * NZL + ll) * NC + cc)

    up, down, far = (y + 1) % NY, (y + 3) % NY, (y + 2) % NY
    dev_up, dev_down = dev(up, zh, x, zl, c), dev(down, zh, x, zl, c)
    partner = dev(y, zh, x, zl, 1 - c)

    loads = [
        pltpu.make_async_copy(gp.at[y], own, load_sem.at[0]),
        pltpu.make_async_copy(gp.at[up, zh], side_p, load_sem.at[1]),
        pltpu.make_async_copy(gp.at[down, 1 - zh], side_m, load_sem.at[2]),
        pltpu.make_async_copy(stats, st, load_sem.at[3]),
        pltpu.make_async_copy(roots, rt, load_sem.at[4]),
    ]
    for copy in loads:
        copy.start()

    barrier = pltpu.get_barrier_semaphore()
    count = 0
    for peer in (dev_up, dev_down, partner):
        pl.semaphore_signal(barrier, inc=1, device_id=peer, device_id_type=MESH)
        count += 1
    for h in range(NZH):
        for k in range(NX):
            for l in range(NZL):
                if (h, k, l) != (0, 0, 0):
                    peer = dev(y, (zh + h) % NZH, (x + k) % NX, (zl + l) % NZL, c)
                    pl.semaphore_signal(barrier, inc=1, device_id=peer, device_id_type=MESH)
                    count += 1
    pl.semaphore_wait(barrier, count)

    def remote(src, dst, send, recv, to):
        copy = pltpu.make_async_remote_copy(
            src_ref=src, dst_ref=dst, send_sem=send, recv_sem=recv, device_id=to, device_id_type=MESH
        )
        copy.start()
        return copy

    y_copies = {}

    def y_send_pair(kind, k):
        xx = (x + ORDER[k]) % NX
        if kind == 0:
            plus, to_p = gp.at[far, zh, xx], r1p.at[k]
            minus, to_m = gp.at[far, 1 - zh, xx], r1m.at[k]
        elif kind == 1:
            plus, to_p = gp.at[up, 1 - zh, xx], r2ap.at[k]
            minus, to_m = gp.at[down, zh, xx], r2am.at[k]
        else:
            plus, to_p = r1p.at[k], r2bp.at[k]
            minus, to_m = r1m.at[k], r2bm.at[k]
        if kind == 2:
            y_copies[0, 0, k].wait_recv()
            r1p[k] = (r1p[k].astype(F32) + side_p[xx].astype(F32)).astype(BF)
        y_copies[kind, 0, k] = remote(plus, to_p, y_send.at[kind, 0, k], y_recv.at[kind, 0, k], dev_up)
        if kind == 2:
            y_copies[0, 1, k].wait_recv()
            r1m[k] = (r1m[k].astype(F32) + side_m[xx].astype(F32)).astype(BF)
        y_copies[kind, 1, k] = remote(minus, to_m, y_send.at[kind, 1, k], y_recv.at[kind, 1, k], dev_down)

    z_copies = {}

    def finish(k):
        xx = (x + ORDER[k]) % NX
        for h in (1, 0):
            zz = (zh + h) % NZH
            direct, chain = (r2am, r2bp) if h == 0 else (r2ap, r2bm)
            y_copies[1, 1 - h, k].wait_recv()
            y_copies[2, h, k].wait_recv()
            total = own[zz, xx].astype(F32) + direct[k].astype(F32) + chain[k].astype(F32)
            own[zz, xx] = total.astype(BF)
            for step in (2, 1, 3, 0):
                l = (zl + step) % NZL
                if (h, ORDER[k], step) == (0, 0, 0):
                    local = pltpu.make_async_copy(own.at[zz, xx, l], zrecv.at[h, k, step], load_sem.at[5])
                    local.start()
                    z_copies[h, k, step] = local
                else:
                    z_copies[h, k, step] = remote(
                        own.at[zz, xx, l], zrecv.at[h, k, step], z_send.at[h, k, step], z_recv.at[h, k, step],
                        dev(y, zz, xx, l, c),
                    )

    y_send_pair(0, 0)
    y_send_pair(0, 1)
    y_send_pair(1, 0)
    loads[1].wait()
    loads[2].wait()
    y_send_pair(2, 0)
    y_send_pair(0, 2)
    y_send_pair(1, 1)
    roots_copy = remote(roots, other, c_send.at[4], c_recv.at[4], partner)
    y_send_pair(2, 1)
    y_send_pair(0, 3)
    y_send_pair(1, 2)
    loads[0].wait()
    finish(0)
    y_send_pair(2, 2)
    y_send_pair(1, 3)
    finish(1)
    y_send_pair(2, 3)
    finish(2)
    finish(3)

    loads[3].wait()
    loads[4].wait()

    c_copies = []
    for k in range(NX):
        xs = (x + NX - ORDER[k]) % NX
        for step in range(NZL):
            ls = (zl + NZL - step) % NZL
            for h in range(NZH):
                if (h, ORDER[k], step) == (0, 0, 0):
                    z_copies[h, k, step].wait()
                else:
                    z_copies[h, k, step].wait_recv()
            total = zrecv[0, k, step].astype(F32) + zrecv[1, k, step].astype(F32)
            gfull[xs, c, ls] = total.astype(BF)
        c_copies.append(remote(gfull.at[xs, c], gfull.at[xs, c], c_send.at[k], c_recv.at[k], partner))
    for copy in c_copies:
        copy.wait_recv()
    roots_copy.wait_recv()

    return_rows = (NX, NC, NZL, ROWS, BS)
    del return_rows
    whole = jnp.concatenate(
        [gfull[a, b, l] for a in range(NX) for l in range(NZL) for b in range(NC)], axis=0
    )
    gw = whole

    def dot(a, b):
        return jnp.dot(a, b, preferred_element_type=F32)

    def do_update(left, right):
        rows = jnp.concatenate([left[pl.ds((2 * j + c) * ROWS, ROWS), :] for j in range(NX * NZL)], axis=0)
        prod[...] = dot(rows, gw).astype(BF)
        upd[...] = dot(prod[...], right[...]).astype(BF).reshape(NX * NZL, ROWS, BS)

    @pl.when(c == 0)
    def _():
        do_update(rt, other)

    @pl.when(c == 1)
    def _():
        do_update(other, rt)

    u_copies = []
    here = x * NZL + zl
    for k in range(NX):
        for step in range(NZL):
            xx, l = (x + ORDER[k]) % NX, (zl + step) % NZL
            j = k * NZL + step
            if (ORDER[k], step) == (0, 0):
                local = pltpu.make_async_copy(upd.at[here], update.at[here], load_sem.at[6])
                local.start()
                u_copies.append(local)
            else:
                u_copies.append(
                    remote(upd.at[xx * NZL + l], update.at[here], u_send.at[j], u_recv.at[j], dev(y, zh, xx, l, c))
                )

    @pl.when(c == 0)
    def _():
        x32[...] = lax.dot_general(gw, gw, (((1,), (1,)), ((), ())), preferred_element_type=F32)

    @pl.when(c == 1)
    def _():
        x32[...] = lax.dot_general(gw, gw, (((0,), (0,)), ((), ())), preferred_element_type=F32)

    fresh = BETA * st[...] + (1.0 - BETA) / BS * x32[...]
    st[...] = fresh
    stats_out = pltpu.make_async_copy(st, new_stats, out_sem.at[0])
    stats_out.start()
    square = jnp.sum(fresh * fresh, axis=0, keepdims=True)
    square = jnp.sum(square, axis=1, keepdims=True) + 1e-6
    inverse = lax.rsqrt(square)
    scale = lax.rsqrt(jnp.sqrt(jnp.sqrt(square)))

    current = st[...] * inverse
    m32[...] = current
    mb[...] = current.astype(BF)
    eye = (
        lax.broadcasted_iota(jnp.int32, (BS, BS), 0) == lax.broadcasted_iota(jnp.int32, (BS, BS), 1)
    ).astype(F32)
    x_now = 1.25 * eye - 0.25 * current
    x32[...] = x_now
    xb[...] = x_now.astype(BF)
    q = 25.0 / 16.0

    def raise_m(first):
        for t in range(0, BS, TILE):
            rows = pl.ds(t, TILE)
            n = (dot(mb[rows, :], mb[...]) - 10.0 * m32[rows, :]) * (1.0 / 16.0)
            n32[rows, :] = n
            nb[rows, :] = n.astype(BF)
        if not first:
            for t in range(0, BS, TILE):
                rows = pl.ds(t, TILE)
                value = 1.25 * x32[rows, :] - 0.25 * dot(xb[rows, :], mb[...])
                x32[rows, :] = value
                xb[rows, :] = value.astype(BF)
        for t in range(0, BS, TILE):
            rows = pl.ds(t, TILE)
            w = 2.0 * q * n32[rows, :] + dot(nb[rows, :], nb[...])
            wb[rows, :] = w.astype(BF)
        for t in range(0, BS, TILE):
            rows = pl.ds(t, TILE)
            m32[rows, :] = q * q * m32[rows, :] + dot(wb[rows, :], mb[...])
        mb[...] = m32[...].astype(BF)

    raise_m(True)

    @pl.loop(0, ITERS - 2)
    def _(_):
        raise_m(False)

    flag = refresh[owner // 2]
    for t in range(0, BS, TILE):
        rows = pl.ds(t, TILE)
        value = 1.25 * x32[rows, :] - 0.25 * dot(xb[rows, :], mb[...])
        value = (value * scale).astype(BF)
        root_out[rows, :] = jnp.where(flag == 1, value, rt[rows, :])
    roots_out = pltpu.make_async_copy(root_out, new_roots, out_sem.at[1])
    roots_out.start()

    for kind in range(3):
        for d in range(2):
            for k in range(NX):
                y_copies[kind, d, k].wait_send()
    for (h, k, step), copy in z_copies.items():
        if (h, ORDER[k], step) != (0, 0, 0):
            copy.wait_send()
    for copy in c_copies:
        copy.wait_send()
    roots_copy.wait_send()
    for copy in u_copies:
        copy.wait()
    stats_out.wait()
    roots_out.wait()


def local(grad_parts, stats, roots, refresh):
    gp = grad_parts.reshape(NY, NZH, NX, NZL, ROWS, BS)
    anywhere = pl.BlockSpec(memory_space=pl.ANY)
    chunk = (NX, NZL, ROWS, BS)
    dma = pltpu.SemaphoreType.DMA
    new_stats, new_roots, update = pl.pallas_call(
        kernel,
        out_shape=(
            jax.ShapeDtypeStruct((BS, BS), F32),
            jax.ShapeDtypeStruct((BS, BS), BF),
            jax.ShapeDtypeStruct((NX * NZL, ROWS, BS), BF),
        ),
        in_specs=[anywhere, anywhere, anywhere, pl.BlockSpec(memory_space=pltpu.SMEM)],
        out_specs=(anywhere, anywhere, anywhere),
        scratch_shapes=[
            pltpu.VMEM((NZH, *chunk), BF),
            *[pltpu.VMEM(chunk, BF) for _ in range(8)],
            pltpu.VMEM((NZH, *chunk), BF),
            pltpu.VMEM((NX, NC, NZL, ROWS, BS), BF),
            pltpu.VMEM((BS, BS), F32),
            pltpu.VMEM((BS, BS), BF),
            pltpu.VMEM((BS, BS), BF),
            pltpu.VMEM((BS, BS), F32),
            pltpu.VMEM((BS, BS), BF),
            pltpu.VMEM((BS, BS), F32),
            pltpu.VMEM((BS, BS), BF),
            pltpu.VMEM((BS, BS), F32),
            pltpu.VMEM((BS, BS), BF),
            pltpu.VMEM((BS, BS), BF),
            pltpu.VMEM((BS // 2, BS), BF),
            pltpu.VMEM((NX * NZL, ROWS, BS), BF),
            pltpu.VMEM((BS, BS), BF),
            dma((7,)),
            dma((3, 2, NX)),
            dma((3, 2, NX)),
            dma((NZH, NX, NZL)),
            dma((NZH, NX, NZL)),
            dma((NX + 1,)),
            dma((NX + 1,)),
            dma((NX * NZL,)),
            dma((NX * NZL,)),
            dma((2,)),
        ],
        compiler_params=pltpu.CompilerParams(
            collective_id=0, has_side_effects=True, vmem_limit_bytes=40 * 1024 * 1024
        ),
        name="shampoo",
    )(gp, stats[0], roots[0], refresh)
    return new_stats[None], new_roots[None], update


def solution(mesh):
    return jax.shard_map(
        local,
        mesh=mesh,
        in_specs=(
            P("dp", None, "owner", None),
            P(("dp", "owner"), None, None),
            P(("dp", "owner"), None, None),
            P("dp"),
        ),
        out_specs=(
            P(("dp", "owner"), None, None),
            P(("dp", "owner"), None, None),
            P("dp", "owner", None),
        ),
        check_vma=False,
    )
```

```python
import jax
import jax.numpy as jnp
from jax import lax
from jax.experimental import pallas as pl
from jax.experimental.pallas import tpu as pltpu
from jax.sharding import PartitionSpec as P

MESH = pl.DeviceIdType.MESH
BF = jnp.bfloat16
F32 = jnp.float32
BS = 512
ITERS = 5
BETA = 0.8
NY, NZH, NX, NZL, NC = 4, 2, 4, 4, 2
NZ = NZH * NZL
ROWS = 16
TILE = 128
PLUS = (4, 3, 2, 0)
MINUS = (5, 6, 7, 1)
HALVES = 2
WIDE = NX // HALVES
CHUNKS = len(PLUS) * HALVES
AHEAD = 3
LAG = 3
SPREAD = tuple((dx, step) for dx in (2, 1, 3, 0) for step in (2, 3, 1, 0))


def kernel(
    gp, stats, roots, flags,
    new_stats, new_roots, update,
    own, near_p, near_m, r1p, r1m, r2ap, r2am, r2bp, r2bm, zrecv, gfull, st, rt, other,
    m32, mb, x32, xb, n32, nb, wb, prod, upd, refresh,
    load_sem, y_send, y_recv, z_send, z_recv, c_send, c_recv, u_send, u_recv,
):
    dp = lax.axis_index("dp")
    owner = lax.axis_index("owner")
    y, zh = dp // NZH, dp % NZH
    x, zl, c = owner // (NZL * NC), (owner // NC) % NZL, owner % NC
    z = zh * NZL + zl

    def dev(yy, zz, xx, cc):
        return (yy * NZH + zz // NZL, (xx * NZL + zz % NZL) * NC + cc)

    up, down, far = (y + 1) % NY, (y + 3) % NY, (y + 2) % NY
    dev_up, dev_down = dev(up, z, x, c), dev(down, z, x, c)
    partner = dev(y, z, x, 1 - c)

    barrier = pltpu.get_barrier_semaphore()

    def greet(peer):
        pl.semaphore_signal(barrier, inc=1, device_id=peer, device_id_type=MESH)

    for peer in (dev_up, dev_down, partner):
        greet(peer)
    for dx in range(NX):
        for dz in range(NZ):
            if (dx, dz) != (0, 0):
                greet(dev(y, (z + dz) % NZ, (x + dx) % NX, c))

    loads = [
        pltpu.make_async_copy(gp.at[up], near_p, load_sem.at[0]),
        pltpu.make_async_copy(gp.at[down], near_m, load_sem.at[1]),
        pltpu.make_async_copy(gp.at[y], own, load_sem.at[2]),
        pltpu.make_async_copy(roots, rt, load_sem.at[3]),
        pltpu.make_async_copy(stats, st, load_sem.at[4]),
        pltpu.make_async_copy(flags, refresh, load_sem.at[5]),
    ]
    for copy in loads:
        copy.start()

    pl.semaphore_wait(barrier, 2 + NX * NZ)

    def remote(src, dst, send, recv, to):
        copy = pltpu.make_async_remote_copy(
            src_ref=src, dst_ref=dst, send_sem=send, recv_sem=recv, device_id=to, device_id_type=MESH
        )
        copy.start()
        return copy

    def part(ref, dz, k):
        zz = (z + dz) % NZ
        return ref.at[zz // NZL, pl.ds(WIDE * (k % HALVES), WIDE), zz % NZL]

    y_copies = {}

    def y_step(kind, k):
        dzp, dzm = PLUS[k // HALVES], MINUS[k // HALVES]
        if kind == 0:
            plus, to_p = part(gp.at[far], dzp, k), r1p.at[k]
            minus, to_m = part(gp.at[far], dzm, k), r1m.at[k]
        elif kind == 1:
            plus, to_p = part(gp.at[up], dzm, k), r2ap.at[k]
            minus, to_m = part(gp.at[down], dzp, k), r2am.at[k]
        else:
            plus, to_p = r1p.at[k], r2bp.at[k]
            minus, to_m = r1m.at[k], r2bm.at[k]
        if kind == 2:
            y_copies[0, 0, k].wait_recv()
            r1p[k] = (r1p[k].astype(F32) + part(near_p, dzp, k)[...].astype(F32)).astype(BF)
        y_copies[kind, 0, k] = remote(plus, to_p, y_send.at[kind, 0, k], y_recv.at[kind, 0, k], dev_up)
        if kind == 2:
            y_copies[0, 1, k].wait_recv()
            r1m[k] = (r1m[k].astype(F32) + part(near_m, dzm, k)[...].astype(F32)).astype(BF)
        y_copies[kind, 1, k] = remote(minus, to_m, y_send.at[kind, 1, k], y_recv.at[kind, 1, k], dev_down)

    z_copies = []

    def finish(k):
        for side in range(2):
            dz = (PLUS, MINUS)[side][k // HALVES]
            direct, chain = ((r2am, r2bp), (r2ap, r2bm))[side]
            y_copies[1, 1 - side, k].wait_recv()
            y_copies[2, side, k].wait_recv()
            block = part(own, dz, k)
            total = block[...].astype(F32) + direct[k].astype(F32) + chain[k].astype(F32)
            block[...] = total.astype(BF)
            zz = (z + dz) % NZ
            for i in range(WIDE):
                xx = WIDE * (k % HALVES) + i
                src, dst = own.at[zz // NZL, xx, zz % NZL], zrecv.at[dz, x]
                copy = pltpu.make_async_remote_copy(
                    src_ref=src, dst_ref=dst, send_sem=z_send.at[dz, xx], recv_sem=z_recv.at[dz, x],
                    device_id=dev(y, zz, xx, c), device_id_type=MESH,
                )
                if dz == 0:
                    @pl.when(xx != x)
                    def _():
                        copy.start()

                    @pl.when(xx == x)
                    def _():
                        zrecv[0, x] = own[zz // NZL, xx, zz % NZL]
                else:
                    copy.start()
                z_copies.append((dz, xx, copy))

    for k in range(AHEAD):
        y_step(0, k)
    y_step(1, 0)
    roots_copy = remote(roots, other, c_send.at[NZL], c_recv.at[NZL], partner)
    loads[0].wait()
    loads[1].wait()
    for k in range(CHUNKS):
        y_step(2, k)
        if k + AHEAD < CHUNKS:
            y_step(0, k + AHEAD)
        if k + 1 < CHUNKS:
            y_step(1, k + 1)
        if k == LAG:
            loads[2].wait()
        if k >= LAG:
            finish(k - LAG)
    for k in range(CHUNKS - LAG, CHUNKS):
        finish(k)

    c_copies = []
    for first in (2, 3, 0, 1):
        ls = (zl + NZL - first) % NZL
        for dz in (first, first + NZL):
            for dx in range(NX):
                xs = (x + dx) % NX
                arrival = pltpu.make_async_remote_copy(
                    src_ref=zrecv.at[dz, xs], dst_ref=zrecv.at[dz, xs], send_sem=z_send.at[dz, 0],
                    recv_sem=z_recv.at[dz, xs], device_id=partner, device_id_type=MESH,
                )
                if (dz, dx) != (0, 0):
                    arrival.wait_recv()
        gfull[:, ls, c] = (zrecv[first].astype(F32) + zrecv[first + NZL].astype(F32)).astype(BF)
        c_copies.append(
            remote(gfull.at[:, ls, c], gfull.at[:, ls, c], c_send.at[first], c_recv.at[first], partner)
        )
    for copy in loads[3:]:
        copy.wait()
    roots_copy.wait_recv()
    for copy in c_copies:
        copy.wait_recv()

    def dot(a, b):
        return jnp.dot(a, b, preferred_element_type=F32)

    def flat(ref):
        return ref[...].reshape(BS, BS)

    for side, left, right in ((0, rt, other), (1, other, rt)):
        @pl.when(c == side)
        def _():
            prod[...] = dot(left[:, side].reshape(BS // NC, BS), flat(gfull)).astype(BF)
            upd[...] = dot(prod[...], flat(right)).astype(BF).reshape(NX * NZL, ROWS, BS)

    u_copies = []
    here = x * NZL + zl
    swaps = (zl, zl + 1 - 2 * (zl % 2), (zl + 2) % NZL, NZL - 1 - zl)
    for dx, step in SPREAD:
        xx, l = (x + dx) % NX, swaps[step]
        j = dx * NZL + step
        if j == 0:
            update[here] = upd[here]
        else:
            u_copies.append(
                remote(upd.at[xx * NZL + l], update.at[here], u_send.at[j], u_recv.at[j], dev(y, zh * NZL + l, xx, c))
            )

    @pl.when(c == 0)
    def _():
        g = flat(gfull)
        x32[...] = lax.dot_general(g, g, (((1,), (1,)), ((), ())), preferred_element_type=F32)

    @pl.when(c == 1)
    def _():
        g = flat(gfull)
        x32[...] = lax.dot_general(g, g, (((0,), (0,)), ((), ())), preferred_element_type=F32)

    fresh = BETA * st[...] + (1.0 - BETA) / BS * x32[...]
    new_stats[...] = fresh
    square = jnp.sum(fresh * fresh, axis=0, keepdims=True)
    square = jnp.sum(square, axis=1, keepdims=True) + 1e-6
    inverse = lax.rsqrt(square)
    scale = lax.rsqrt(jnp.sqrt(jnp.sqrt(square)))

    current = new_stats[...] * inverse
    m32[...] = current
    mb[...] = current.astype(BF)
    eye = (
        lax.broadcasted_iota(jnp.int32, (BS, BS), 0) == lax.broadcasted_iota(jnp.int32, (BS, BS), 1)
    ).astype(F32)
    x_now = 1.25 * eye - 0.25 * current
    x32[...] = x_now
    xb[...] = x_now.astype(BF)
    q = 25.0 / 16.0

    def raise_m(first):
        for t in range(0, BS, TILE):
            rows = pl.ds(t, TILE)
            n = (dot(mb[rows, :], mb[...]) - 10.0 * m32[rows, :]) * (1.0 / 16.0)
            n32[rows, :] = n
            nb[rows, :] = n.astype(BF)
        if not first:
            for t in range(0, BS, TILE):
                rows = pl.ds(t, TILE)
                value = 1.25 * x32[rows, :] - 0.25 * dot(xb[rows, :], mb[...])
                x32[rows, :] = value
                xb[rows, :] = value.astype(BF)
        for t in range(0, BS, TILE):
            rows = pl.ds(t, TILE)
            w = 2.0 * q * n32[rows, :] + dot(nb[rows, :], nb[...])
            wb[rows, :] = w.astype(BF)
        for t in range(0, BS, TILE):
            rows = pl.ds(t, TILE)
            m32[rows, :] = q * q * m32[rows, :] + dot(wb[rows, :], mb[...])
        mb[...] = m32[...].astype(BF)

    raise_m(True)

    @pl.loop(0, ITERS - 2)
    def _(_):
        raise_m(False)

    flag = refresh[owner // NC]
    old = flat(rt)
    value = 1.25 * x32[...] - 0.25 * dot(xb[...], mb[...])
    new_roots[...] = jnp.where(flag == 1, (value * scale).astype(BF), old)

    for copy in y_copies.values():
        copy.wait_send()
    for dz, xx, copy in z_copies:
        if dz == 0:
            @pl.when(xx != x)
            def _():
                copy.wait_send()
        else:
            copy.wait_send()
    for copy in c_copies:
        copy.wait_send()
    roots_copy.wait_send()
    for copy in u_copies:
        copy.wait()


def write_out(a, b, d, a_out, b_out, d_out, sems):
    copies = [
        pltpu.make_async_copy(src, dst, sems.at[i])
        for i, (src, dst) in enumerate(((a, a_out), (b, b_out), (d, d_out)))
    ]
    for copy in copies:
        copy.start()
    for copy in copies:
        copy.wait()


def local(grad_parts, stats, roots, refresh):
    here = tuple(
        pltpu.with_memory_space_constraint(value, pltpu.HBM)
        for value in (
            grad_parts.reshape(NY, NZH, NX, NZL, ROWS, BS),
            stats[0],
            roots.reshape(NX * NZL, NC, ROWS, BS),
            refresh,
        )
    )
    hbm = pl.BlockSpec(memory_space=pltpu.HBM)
    vmem = pl.BlockSpec(memory_space=pltpu.VMEM)
    everything = (NZH, NX, NZL, ROWS, BS)
    pieces = (CHUNKS, WIDE, ROWS, BS)
    whole = (NX * NZL, NC, ROWS, BS)
    square = (BS, BS)
    dma = pltpu.SemaphoreType.DMA
    outs = ((square, F32), (square, BF), ((NX * NZL, ROWS, BS), BF))
    done = pl.pallas_call(
        kernel,
        out_shape=tuple(pltpu.VMEM(shape, kind) for shape, kind in outs),
        in_specs=[hbm] * 4,
        out_specs=(vmem,) * 3,
        scratch_shapes=[
            *[pltpu.VMEM(everything, BF) for _ in range(3)],
            *[pltpu.VMEM(pieces, BF) for _ in range(6)],
            pltpu.VMEM((NZ, NX, ROWS, BS), BF),
            pltpu.VMEM((NX, NZL, NC, ROWS, BS), BF),
            pltpu.VMEM(square, F32),
            pltpu.VMEM(whole, BF),
            pltpu.VMEM(whole, BF),
            pltpu.VMEM(square, F32),
            pltpu.VMEM(square, BF),
            pltpu.VMEM(square, F32),
            pltpu.VMEM(square, BF),
            pltpu.VMEM(square, F32),
            pltpu.VMEM(square, BF),
            pltpu.VMEM(square, BF),
            pltpu.VMEM((BS // NC, BS), BF),
            pltpu.VMEM((NX * NZL, ROWS, BS), BF),
            pltpu.SMEM((NX * NZL,), jnp.int32),
            dma((6,)),
            dma((3, 2, CHUNKS)),
            dma((3, 2, CHUNKS)),
            dma((NZ, NX)),
            dma((NZ, NX)),
            dma((NZL + 1,)),
            dma((NZL + 1,)),
            dma((NX * NZL,)),
            dma((NX * NZL,)),
        ],
        compiler_params=pltpu.CompilerParams(
            collective_id=0, has_side_effects=True, vmem_limit_bytes=40 * 1024 * 1024
        ),
        name="shampoo",
    )(*here)
    new_stats, new_roots, update = pl.pallas_call(
        write_out,
        out_shape=tuple(pltpu.HBM(shape, kind) for shape, kind in outs),
        in_specs=[vmem] * 3,
        out_specs=(hbm,) * 3,
        scratch_shapes=[dma((3,))],
        name="write_out",
    )(*(pltpu.with_memory_space_constraint(value, pltpu.VMEM) for value in done))
    return new_stats[None], new_roots[None], update


def solution(mesh):
    placed = (
        P("dp", None, "owner", None),
        P(("dp", "owner"), None, None),
        P(("dp", "owner"), None, None),
        P("dp"),
    )
    return jax.shard_map(
        local,
        mesh=mesh,
        in_specs=placed,
        out_specs=(
            P(("dp", "owner"), None, None),
            P(("dp", "owner"), None, None),
            P("dp", "owner", None),
        ),
        check_vma=False,
    )
```

```python
import jax
import jax.numpy as jnp
from jax import lax
from jax.experimental import pallas as pl
from jax.experimental.pallas import tpu as pltpu
from jax.sharding import PartitionSpec as P

MESH = pl.DeviceIdType.MESH
BF = jnp.bfloat16
F32 = jnp.float32
BS = 512
ITERS = 5
BETA = 0.8
NY, NZH, NX, NZL, NC = 4, 2, 4, 4, 2
NZ = NZH * NZL
ROWS = 16
TILE = 128
PLUS = (((1, 0), (0, 3), (0, 0), (1, 1)), ((1, 0), (1, 1), (0, 2), (0, 0)))
MINUS = (((1, 2), (0, 2), (0, 1), (1, 3)), ((1, 2), (1, 3), (0, 3), (0, 1)))
HALVES = 2
WIDE = NX // HALVES
CHUNKS = len(PLUS[0]) * HALVES
AHEAD = 3
ROUNDS = ((0,), (1,), (2,), (3, 4), (), (), (), ())
LAG = 3
SPREAD = tuple((dx, step) for dx in (2, 1, 3, 0) for step in (2, 3, 1, 0))


def kernel(
    gp, stats, roots, flags,
    new_stats, new_roots, update,
    own, near_p, near_m, r1p, r1m, r2ap, r2am, r2bp, r2bm, zrecv, gfull, st, rt, other,
    m32, mb, x32, xb, n32, nb, wb, prod, upd, refresh,
    load_sem, y_send, y_recv, z_send, z_recv, c_send, c_recv, u_send, u_recv, ring,
):
    dp = lax.axis_index("dp")
    owner = lax.axis_index("owner")
    y, zh = dp // NZH, dp % NZH
    x, zl, c = owner // (NZL * NC), (owner // NC) % NZL, owner % NC
    z = zh * NZL + zl

    def dev(yy, zz, xx, cc):
        return (yy * NZH + zz // NZL, (xx * NZL + zz % NZL) * NC + cc)

    up, down, far = (y + 1) % NY, (y + 3) % NY, (y + 2) % NY
    dev_up, dev_down = dev(up, z, x, c), dev(down, z, x, c)
    partner = dev(y, z, x, 1 - c)

    barrier = pltpu.get_barrier_semaphore()

    def greet(peer):
        pl.semaphore_signal(barrier, inc=1, device_id=peer, device_id_type=MESH)

    z_pair = (dev(y, (z + 1) % NZ, x, c), dev(y, (z + NZ - 1) % NZ, x, c))
    x_pair = (dev(y, z, (x + 1) % NX, c), dev(y, z, (x + NX - 1) % NX, c))
    for peer in (dev_up, dev_down, partner, *z_pair, *x_pair):
        greet(peer)

    loads = [
        pltpu.make_async_copy(gp.at[up], near_p, load_sem.at[0]),
        pltpu.make_async_copy(gp.at[down], near_m, load_sem.at[1]),
        pltpu.make_async_copy(gp.at[y], own, load_sem.at[2]),
        pltpu.make_async_copy(roots, rt, load_sem.at[3]),
        pltpu.make_async_copy(stats, st, load_sem.at[4]),
        pltpu.make_async_copy(flags, refresh, load_sem.at[5]),
    ]
    for copy in loads:
        copy.start()

    pl.semaphore_wait(barrier, 7)

    rounds = (z_pair, z_pair, z_pair, x_pair, x_pair)

    def tell(i):
        for peer in rounds[i]:
            pl.semaphore_signal(ring.at[i], inc=1, device_id=peer, device_id_type=MESH)

    def hear(i):
        pl.semaphore_wait(ring.at[i], 2)

    def remote(src, dst, send, recv, to):
        copy = pltpu.make_async_remote_copy(
            src_ref=src, dst_ref=dst, send_sem=send, recv_sem=recv, device_id=to, device_id_type=MESH
        )
        copy.start()
        return copy

    def offset(table, k):
        (h0, s0), (h1, s1) = table[0][k // HALVES], table[1][k // HALVES]
        return h0 + zh * (h1 - h0), s0 + zh * (s1 - s0)

    def place(off):
        return (zh + off[0]) % NZH, (zl + off[1]) % NZL

    def part(ref, off, k):
        zzh, zzl = place(off)
        return ref.at[zzh, pl.ds(WIDE * (k % HALVES), WIDE), zzl]

    y_copies = {}

    def y_step(kind, k):
        dzp, dzm = offset(PLUS, k), offset(MINUS, k)
        if kind == 0:
            plus, to_p = part(gp.at[far], dzp, k), r1p.at[k]
            minus, to_m = part(gp.at[far], dzm, k), r1m.at[k]
        elif kind == 1:
            plus, to_p = part(gp.at[up], dzm, k), r2ap.at[k]
            minus, to_m = part(gp.at[down], dzp, k), r2am.at[k]
        else:
            plus, to_p = r1p.at[k], r2bp.at[k]
            minus, to_m = r1m.at[k], r2bm.at[k]
        if kind == 2:
            y_copies[0, 0, k].wait_recv()
            r1p[k] = (r1p[k].astype(F32) + part(near_p, dzp, k)[...].astype(F32)).astype(BF)
        y_copies[kind, 0, k] = remote(plus, to_p, y_send.at[kind, 0, k], y_recv.at[kind, 0, k], dev_up)
        if kind == 2:
            y_copies[0, 1, k].wait_recv()
            r1m[k] = (r1m[k].astype(F32) + part(near_m, dzm, k)[...].astype(F32)).astype(BF)
        y_copies[kind, 1, k] = remote(minus, to_m, y_send.at[kind, 1, k], y_recv.at[kind, 1, k], dev_down)

    z_copies = []

    def finish(k):
        for side in range(2):
            table = (PLUS, MINUS)[side]
            off = offset(table, k)
            direct, chain = ((r2am, r2bp), (r2ap, r2bm))[side]
            y_copies[1, 1 - side, k].wait_recv()
            y_copies[2, side, k].wait_recv()
            block = part(own, off, k)
            total = block[...].astype(F32) + direct[k].astype(F32) + chain[k].astype(F32)
            block[...] = total.astype(BF)
            zzh, zzl = place(off)
            for i in range(WIDE):
                xx = WIDE * (k % HALVES) + i
                copy = pltpu.make_async_remote_copy(
                    src_ref=own.at[zzh, xx, zzl], dst_ref=zrecv.at[off[0], off[1], x],
                    send_sem=z_send.at[side, k, i], recv_sem=z_recv.at[off[0], off[1], x],
                    device_id=dev(y, zzh * NZL + zzl, xx, c), device_id_type=MESH,
                )
                if (0, 0) in (table[0][k // HALVES], table[1][k // HALVES]):
                    stays = jnp.logical_and(jnp.logical_and(off[0] == 0, off[1] == 0), xx == x)

                    @pl.when(jnp.logical_not(stays))
                    def _():
                        copy.start()

                    @pl.when(stays)
                    def _():
                        zrecv[0, 0, x] = own[zzh, xx, zzl]
                else:
                    stays = None
                    copy.start()
                z_copies.append((stays, copy))

    for k in range(AHEAD):
        y_step(0, k)
    y_step(1, 0)
    roots_copy = remote(roots, other, c_send.at[NZL], c_recv.at[NZL], partner)
    tell(0)
    loads[0].wait()
    loads[1].wait()
    for k in range(CHUNKS):
        y_step(2, k)
        if k + AHEAD < CHUNKS:
            y_step(0, k + AHEAD)
        if k + 1 < CHUNKS:
            y_step(1, k + 1)
        for i in ROUNDS[k]:
            hear(i)
            if i + 1 < len(rounds):
                tell(i + 1)
        if k == LAG:
            loads[2].wait()
        if k >= LAG:
            finish(k - LAG)
    for k in range(CHUNKS - LAG, CHUNKS):
        finish(k)

    c_copies = []
    for step in (2, 3, 0, 1):
        ls = (zl + NZL - step) % NZL
        for h in range(NZH):
            for dx in range(NX):
                xs = (x + dx) % NX
                arrival = pltpu.make_async_remote_copy(
                    src_ref=zrecv.at[h, step, xs], dst_ref=zrecv.at[h, step, xs], send_sem=z_send.at[0, 0, 0],
                    recv_sem=z_recv.at[h, step, xs], device_id=partner, device_id_type=MESH,
                )
                if (h, step, dx) != (0, 0, 0):
                    arrival.wait_recv()
        gfull[:, ls, c] = (zrecv[0, step].astype(F32) + zrecv[1, step].astype(F32)).astype(BF)
        c_copies.append(
            remote(gfull.at[:, ls, c], gfull.at[:, ls, c], c_send.at[step], c_recv.at[step], partner)
        )
    for copy in loads[3:]:
        copy.wait()
    roots_copy.wait_recv()
    for copy in c_copies:
        copy.wait_recv()

    def dot(a, b):
        return jnp.dot(a, b, preferred_element_type=F32)

    def flat(ref):
        return ref[...].reshape(BS, BS)

    for side, left, right in ((0, rt, other), (1, other, rt)):
        @pl.when(c == side)
        def _():
            prod[...] = dot(left[:, side].reshape(BS // NC, BS), flat(gfull)).astype(BF)
            upd[...] = dot(prod[...], flat(right)).astype(BF).reshape(NX * NZL, ROWS, BS)

    u_copies = []
    here = x * NZL + zl
    swaps = (zl, zl + 1 - 2 * (zl % 2), (zl + 2) % NZL, NZL - 1 - zl)
    for dx, step in SPREAD:
        xx, l = (x + dx) % NX, swaps[step]
        j = dx * NZL + step
        if j == 0:
            update[here] = upd[here]
        else:
            u_copies.append(
                remote(upd.at[xx * NZL + l], update.at[here], u_send.at[j], u_recv.at[j], dev(y, zh * NZL + l, xx, c))
            )

    @pl.when(c == 0)
    def _():
        g = flat(gfull)
        x32[...] = lax.dot_general(g, g, (((1,), (1,)), ((), ())), preferred_element_type=F32)

    @pl.when(c == 1)
    def _():
        g = flat(gfull)
        x32[...] = lax.dot_general(g, g, (((0,), (0,)), ((), ())), preferred_element_type=F32)

    fresh = BETA * st[...] + (1.0 - BETA) / BS * x32[...]
    new_stats[...] = fresh
    square = jnp.sum(fresh * fresh, axis=0, keepdims=True)
    square = jnp.sum(square, axis=1, keepdims=True) + 1e-6
    inverse = lax.rsqrt(square)
    scale = lax.rsqrt(jnp.sqrt(jnp.sqrt(square)))

    current = new_stats[...] * inverse
    m32[...] = current
    mb[...] = current.astype(BF)
    eye = (
        lax.broadcasted_iota(jnp.int32, (BS, BS), 0) == lax.broadcasted_iota(jnp.int32, (BS, BS), 1)
    ).astype(F32)
    x_now = 1.25 * eye - 0.25 * current
    x32[...] = x_now
    xb[...] = x_now.astype(BF)
    q = 25.0 / 16.0

    def raise_m(first):
        for t in range(0, BS, TILE):
            rows = pl.ds(t, TILE)
            n = (dot(mb[rows, :], mb[...]) - 10.0 * m32[rows, :]) * (1.0 / 16.0)
            n32[rows, :] = n
            nb[rows, :] = n.astype(BF)
        if not first:
            for t in range(0, BS, TILE):
                rows = pl.ds(t, TILE)
                value = 1.25 * x32[rows, :] - 0.25 * dot(xb[rows, :], mb[...])
                x32[rows, :] = value
                xb[rows, :] = value.astype(BF)
        for t in range(0, BS, TILE):
            rows = pl.ds(t, TILE)
            w = 2.0 * q * n32[rows, :] + dot(nb[rows, :], nb[...])
            wb[rows, :] = w.astype(BF)
        for t in range(0, BS, TILE):
            rows = pl.ds(t, TILE)
            m32[rows, :] = q * q * m32[rows, :] + dot(wb[rows, :], mb[...])
        mb[...] = m32[...].astype(BF)

    raise_m(True)

    @pl.loop(0, ITERS - 2)
    def _(_):
        raise_m(False)

    flag = refresh[owner // NC]
    old = flat(rt)
    value = 1.25 * x32[...] - 0.25 * dot(xb[...], mb[...])
    new_roots[...] = jnp.where(flag == 1, (value * scale).astype(BF), old)

    for copy in y_copies.values():
        copy.wait_send()
    for stays, copy in z_copies:
        if stays is None:
            copy.wait_send()
        else:
            @pl.when(jnp.logical_not(stays))
            def _():
                copy.wait_send()
    for copy in c_copies:
        copy.wait_send()
    roots_copy.wait_send()
    for copy in u_copies:
        copy.wait()


def write_out(a, b, d, a_out, b_out, d_out, sems):
    copies = [
        pltpu.make_async_copy(src, dst, sems.at[i])
        for i, (src, dst) in enumerate(((a, a_out), (b, b_out), (d, d_out)))
    ]
    for copy in copies:
        copy.start()
    for copy in copies:
        copy.wait()


def local(grad_parts, stats, roots, refresh):
    here = tuple(
        pltpu.with_memory_space_constraint(value, pltpu.HBM)
        for value in (
            grad_parts.reshape(NY, NZH, NX, NZL, ROWS, BS),
            stats[0],
            roots.reshape(NX * NZL, NC, ROWS, BS),
            refresh,
        )
    )
    hbm = pl.BlockSpec(memory_space=pltpu.HBM)
    vmem = pl.BlockSpec(memory_space=pltpu.VMEM)
    everything = (NZH, NX, NZL, ROWS, BS)
    pieces = (CHUNKS, WIDE, ROWS, BS)
    whole = (NX * NZL, NC, ROWS, BS)
    square = (BS, BS)
    dma = pltpu.SemaphoreType.DMA
    outs = ((square, F32), (square, BF), ((NX * NZL, ROWS, BS), BF))
    done = pl.pallas_call(
        kernel,
        out_shape=tuple(pltpu.VMEM(shape, kind) for shape, kind in outs),
        in_specs=[hbm] * 4,
        out_specs=(vmem,) * 3,
        scratch_shapes=[
            *[pltpu.VMEM(everything, BF) for _ in range(3)],
            *[pltpu.VMEM(pieces, BF) for _ in range(6)],
            pltpu.VMEM((NZH, NZL, NX, ROWS, BS), BF),
            pltpu.VMEM((NX, NZL, NC, ROWS, BS), BF),
            pltpu.VMEM(square, F32),
            pltpu.VMEM(whole, BF),
            pltpu.VMEM(whole, BF),
            pltpu.VMEM(square, F32),
            pltpu.VMEM(square, BF),
            pltpu.VMEM(square, F32),
            pltpu.VMEM(square, BF),
            pltpu.VMEM(square, F32),
            pltpu.VMEM(square, BF),
            pltpu.VMEM(square, BF),
            pltpu.VMEM((BS // NC, BS), BF),
            pltpu.VMEM((NX * NZL, ROWS, BS), BF),
            pltpu.SMEM((NX * NZL,), jnp.int32),
            dma((6,)),
            dma((3, 2, CHUNKS)),
            dma((3, 2, CHUNKS)),
            dma((2, CHUNKS, WIDE)),
            dma((NZH, NZL, NX)),
            dma((NZL + 1,)),
            dma((NZL + 1,)),
            dma((NX * NZL,)),
            dma((NX * NZL,)),
            pltpu.SemaphoreType.REGULAR((5,)),
        ],
        compiler_params=pltpu.CompilerParams(
            collective_id=0, has_side_effects=True, vmem_limit_bytes=40 * 1024 * 1024
        ),
        name="shampoo",
    )(*here)
    new_stats, new_roots, update = pl.pallas_call(
        write_out,
        out_shape=tuple(pltpu.HBM(shape, kind) for shape, kind in outs),
        in_specs=[vmem] * 3,
        out_specs=(hbm,) * 3,
        scratch_shapes=[dma((3,))],
        name="write_out",
    )(*(pltpu.with_memory_space_constraint(value, pltpu.VMEM) for value in done))
    return new_stats[None], new_roots[None], update


def solution(mesh):
    placed = (
        P("dp", None, "owner", None),
        P(("dp", "owner"), None, None),
        P(("dp", "owner"), None, None),
        P("dp"),
    )
    return jax.shard_map(
        local,
        mesh=mesh,
        in_specs=placed,
        out_specs=(
            P(("dp", "owner"), None, None),
            P(("dp", "owner"), None, None),
            P("dp", "owner", None),
        ),
        check_vma=False,
    )
```

```python
import jax
import jax.numpy as jnp
from jax import lax
from jax.experimental import pallas as pl
from jax.experimental.pallas import tpu as pltpu
from jax.sharding import PartitionSpec as P

MESH = pl.DeviceIdType.MESH
BF = jnp.bfloat16
F32 = jnp.float32
BS = 512
ITERS = 5
BETA = 0.8
NY, NZH, NX, NZL, NC = 4, 2, 4, 4, 2
NZ = NZH * NZL
ROWS = 16
TILE = 128
PLUS = (((1, 0), (0, 3), (0, 0), (1, 1)), ((1, 0), (1, 1), (0, 2), (0, 0)))
MINUS = (((1, 2), (0, 2), (0, 1), (1, 3)), ((1, 2), (1, 3), (0, 3), (0, 1)))
HALVES = 2
WIDE = NX // HALVES
CHUNKS = len(PLUS[0]) * HALVES
AHEAD = 4
SWAP = 4
LOADS = 2
EARLY = (0,)
ROUNDS = ((1,), (2,), (3, 4), (), (), (), (), ())
LAG = 2
SPREAD = tuple((dx, step) for dx in (2, 1, 3, 0) for step in (2, 3, 1, 0))


def kernel(
    gp, stats, roots, flags,
    new_stats, new_roots, update,
    own, near_p, near_m, r1p, r1m, r2ap, r2am, r2bp, r2bm, zrecv, gfull, st, rt, other,
    m32, mb, x32, xb, n32, nb, wb, prod, upd, refresh,
    load_sem, y_send, y_recv, z_send, z_recv, c_send, c_recv, u_send, u_recv, ring,
):
    dp = lax.axis_index("dp")
    owner = lax.axis_index("owner")
    y, zh = dp // NZH, dp % NZH
    x, zl, c = owner // (NZL * NC), (owner // NC) % NZL, owner % NC
    z = zh * NZL + zl

    def dev(yy, zz, xx, cc):
        return (yy * NZH + zz // NZL, (xx * NZL + zz % NZL) * NC + cc)

    up, down, far = (y + 1) % NY, (y + 3) % NY, (y + 2) % NY
    dev_up, dev_down = dev(up, z, x, c), dev(down, z, x, c)
    partner = dev(y, z, x, 1 - c)

    barrier = pltpu.get_barrier_semaphore()

    def greet(peer):
        pl.semaphore_signal(barrier, inc=1, device_id=peer, device_id_type=MESH)

    def along_z(d):
        return (z + d < NZ, dev(y, (z + d) % NZ, x, c)), (z >= d, dev(y, (z + NZ - d) % NZ, x, c))

    def along_x(d):
        return (x + d < NX, dev(y, z, (x + d) % NX, c)), (x >= d, dev(y, z, (x + NX - d) % NX, c))

    def present(pairs):
        return sum(lax.convert_element_type(there, jnp.int32) for there, _ in pairs)

    def signal_all(pairs, sem):
        for there, peer in pairs:
            @pl.when(there)
            def _():
                pl.semaphore_signal(sem, inc=1, device_id=peer, device_id_type=MESH)

    for peer in (dev_up, dev_down, partner):
        greet(peer)
    close = (*along_z(1), *along_x(1))
    signal_all(close, barrier)

    loads = [
        pltpu.make_async_copy(gp.at[up], near_p, load_sem.at[0]),
        pltpu.make_async_copy(gp.at[down], near_m, load_sem.at[1]),
        pltpu.make_async_copy(gp.at[y], own, load_sem.at[2]),
        pltpu.make_async_copy(roots, rt, load_sem.at[3]),
        pltpu.make_async_copy(stats, st, load_sem.at[4]),
        pltpu.make_async_copy(flags, refresh, load_sem.at[5]),
    ]
    for copy in loads[:LOADS]:
        copy.start()

    pl.semaphore_wait(barrier, 3 + present(close))

    rounds = (along_z(1), along_z(2), along_z(4), along_x(1), along_x(2))

    def tell(i):
        signal_all(rounds[i], ring.at[i])

    def hear(i):
        pl.semaphore_wait(ring.at[i], present(rounds[i]))

    def remote(src, dst, send, recv, to):
        copy = pltpu.make_async_remote_copy(
            src_ref=src, dst_ref=dst, send_sem=send, recv_sem=recv, device_id=to, device_id_type=MESH
        )
        copy.start()
        return copy

    def offset(table, k):
        (h0, s0), (h1, s1) = table[0][k // HALVES], table[1][k // HALVES]
        return h0 + zh * (h1 - h0), s0 + zh * (s1 - s0)

    def place(off):
        return (zh + off[0]) % NZH, (zl + off[1]) % NZL

    def part(ref, off, k):
        zzh, zzl = place(off)
        return ref.at[zzh, pl.ds(WIDE * (k % HALVES), WIDE), zzl]

    y_copies = {}

    def y_step(kind, k):
        dzp, dzm = offset(PLUS, k), offset(MINUS, k)
        if kind == 0:
            plus, to_p = part(gp.at[far], dzp, k), r1p.at[k]
            minus, to_m = part(gp.at[far], dzm, k), r1m.at[k]
        elif kind == 1:
            plus, to_p = part(gp.at[up], dzm, k), r2ap.at[k]
            minus, to_m = part(gp.at[down], dzp, k), r2am.at[k]
        else:
            plus, to_p = r1p.at[k], r2bp.at[k]
            minus, to_m = r1m.at[k], r2bm.at[k]
        if kind == 2:
            y_copies[0, 0, k].wait_recv()
            r1p[k] = (r1p[k].astype(F32) + part(near_p, dzp, k)[...].astype(F32)).astype(BF)
        y_copies[kind, 0, k] = remote(plus, to_p, y_send.at[kind, 0, k], y_recv.at[kind, 0, k], dev_up)
        if kind == 2:
            y_copies[0, 1, k].wait_recv()
            r1m[k] = (r1m[k].astype(F32) + part(near_m, dzm, k)[...].astype(F32)).astype(BF)
        y_copies[kind, 1, k] = remote(minus, to_m, y_send.at[kind, 1, k], y_recv.at[kind, 1, k], dev_down)

    z_copies = []

    def finish(k):
        for side in range(2):
            table = (PLUS, MINUS)[side]
            off = offset(table, k)
            direct, chain = ((r2am, r2bp), (r2ap, r2bm))[side]
            y_copies[1, 1 - side, k].wait_recv()
            y_copies[2, side, k].wait_recv()
            block = part(own, off, k)
            total = block[...].astype(F32) + direct[k].astype(F32) + chain[k].astype(F32)
            block[...] = total.astype(BF)
            zzh, zzl = place(off)
            for i in range(WIDE):
                xx = WIDE * (k % HALVES) + i
                copy = pltpu.make_async_remote_copy(
                    src_ref=own.at[zzh, xx, zzl], dst_ref=zrecv.at[off[0], off[1], x],
                    send_sem=z_send.at[side, k, i], recv_sem=z_recv.at[off[0], off[1], x],
                    device_id=dev(y, zzh * NZL + zzl, xx, c), device_id_type=MESH,
                )
                if (0, 0) in (table[0][k // HALVES], table[1][k // HALVES]):
                    stays = jnp.logical_and(jnp.logical_and(off[0] == 0, off[1] == 0), xx == x)

                    @pl.when(jnp.logical_not(stays))
                    def _():
                        copy.start()

                    @pl.when(stays)
                    def _():
                        zrecv[0, 0, x] = own[zzh, xx, zzl]
                else:
                    stays = None
                    copy.start()
                z_copies.append((stays, copy))

    for k in range(AHEAD):
        y_step(0, k)
    y_step(1, 0)
    tell(0)
    loads[0].wait()
    loads[1].wait()
    for i in EARLY:
        hear(i)
        tell(i + 1)
    for k in range(CHUNKS):
        if k == 0:
            for copy in loads[LOADS:]:
                copy.start()
        y_step(2, k)
        if k + AHEAD < CHUNKS:
            y_step(0, k + AHEAD)
        if k + 1 < CHUNKS:
            y_step(1, k + 1)
        for i in ROUNDS[k]:
            hear(i)
            if i + 1 < len(rounds):
                tell(i + 1)
        if k == LAG:
            loads[2].wait()
        if k == SWAP:
            roots_copy = remote(roots, other, c_send.at[NZL], c_recv.at[NZL], partner)
        if k >= LAG:
            finish(k - LAG)
    for k in range(CHUNKS - LAG, CHUNKS):
        finish(k)

    c_copies = []
    for step in (2, 3, 0, 1):
        ls = (zl + NZL - step) % NZL
        for h in range(NZH):
            for dx in range(NX):
                xs = (x + dx) % NX
                arrival = pltpu.make_async_remote_copy(
                    src_ref=zrecv.at[h, step, xs], dst_ref=zrecv.at[h, step, xs], send_sem=z_send.at[0, 0, 0],
                    recv_sem=z_recv.at[h, step, xs], device_id=partner, device_id_type=MESH,
                )
                if (h, step, dx) != (0, 0, 0):
                    arrival.wait_recv()
        gfull[:, ls, c] = (zrecv[0, step].astype(F32) + zrecv[1, step].astype(F32)).astype(BF)
        c_copies.append(
            remote(gfull.at[:, ls, c], gfull.at[:, ls, c], c_send.at[step], c_recv.at[step], partner)
        )
    for copy in loads[3:]:
        copy.wait()
    roots_copy.wait_recv()
    for copy in c_copies:
        copy.wait_recv()

    def dot(a, b):
        return jnp.dot(a, b, preferred_element_type=F32)

    def flat(ref):
        return ref[...].reshape(BS, BS)

    for side, left, right in ((0, rt, other), (1, other, rt)):
        @pl.when(c == side)
        def _():
            prod[...] = dot(left[:, side].reshape(BS // NC, BS), flat(gfull)).astype(BF)
            upd[...] = dot(prod[...], flat(right)).astype(BF).reshape(NX * NZL, ROWS, BS)

    u_copies = []
    here = x * NZL + zl
    swaps = (zl, zl + 1 - 2 * (zl % 2), (zl + 2) % NZL, NZL - 1 - zl)
    for dx, step in SPREAD:
        xx, l = (x + dx) % NX, swaps[step]
        j = dx * NZL + step
        if j == 0:
            update[here] = upd[here]
        else:
            u_copies.append(
                remote(upd.at[xx * NZL + l], update.at[here], u_send.at[j], u_recv.at[j], dev(y, zh * NZL + l, xx, c))
            )

    @pl.when(c == 0)
    def _():
        g = flat(gfull)
        x32[...] = lax.dot_general(g, g, (((1,), (1,)), ((), ())), preferred_element_type=F32)

    @pl.when(c == 1)
    def _():
        g = flat(gfull)
        x32[...] = lax.dot_general(g, g, (((0,), (0,)), ((), ())), preferred_element_type=F32)

    fresh = BETA * st[...] + (1.0 - BETA) / BS * x32[...]
    new_stats[...] = fresh
    square = jnp.sum(fresh * fresh, axis=0, keepdims=True)
    square = jnp.sum(square, axis=1, keepdims=True) + 1e-6
    inverse = lax.rsqrt(square)
    scale = lax.rsqrt(jnp.sqrt(jnp.sqrt(square)))

    current = new_stats[...] * inverse
    m32[...] = current
    mb[...] = current.astype(BF)
    eye = (
        lax.broadcasted_iota(jnp.int32, (BS, BS), 0) == lax.broadcasted_iota(jnp.int32, (BS, BS), 1)
    ).astype(F32)
    x_now = 1.25 * eye - 0.25 * current
    x32[...] = x_now
    xb[...] = x_now.astype(BF)
    q = 25.0 / 16.0

    def raise_m(first):
        for t in range(0, BS, TILE):
            rows = pl.ds(t, TILE)
            n = (dot(mb[rows, :], mb[...]) - 10.0 * m32[rows, :]) * (1.0 / 16.0)
            n32[rows, :] = n
            nb[rows, :] = n.astype(BF)
        if not first:
            for t in range(0, BS, TILE):
                rows = pl.ds(t, TILE)
                value = 1.25 * x32[rows, :] - 0.25 * dot(xb[rows, :], mb[...])
                x32[rows, :] = value
                xb[rows, :] = value.astype(BF)
        for t in range(0, BS, TILE):
            rows = pl.ds(t, TILE)
            w = 2.0 * q * n32[rows, :] + dot(nb[rows, :], nb[...])
            wb[rows, :] = w.astype(BF)
        for t in range(0, BS, TILE):
            rows = pl.ds(t, TILE)
            m32[rows, :] = q * q * m32[rows, :] + dot(wb[rows, :], mb[...])
        mb[...] = m32[...].astype(BF)

    raise_m(True)

    @pl.loop(0, ITERS - 2)
    def _(_):
        raise_m(False)

    flag = refresh[owner // NC]
    old = flat(rt)
    value = 1.25 * x32[...] - 0.25 * dot(xb[...], mb[...])
    new_roots[...] = jnp.where(flag == 1, (value * scale).astype(BF), old)

    for copy in y_copies.values():
        copy.wait_send()
    for stays, copy in z_copies:
        if stays is None:
            copy.wait_send()
        else:
            @pl.when(jnp.logical_not(stays))
            def _():
                copy.wait_send()
    for copy in c_copies:
        copy.wait_send()
    roots_copy.wait_send()
    for copy in u_copies:
        copy.wait()


def write_out(a, b, d, a_out, b_out, d_out, sems):
    copies = [
        pltpu.make_async_copy(src, dst, sems.at[i])
        for i, (src, dst) in enumerate(((a, a_out), (b, b_out), (d, d_out)))
    ]
    for copy in copies:
        copy.start()
    for copy in copies:
        copy.wait()


def local(grad_parts, stats, roots, refresh):
    here = tuple(
        pltpu.with_memory_space_constraint(value, pltpu.HBM)
        for value in (
            grad_parts.reshape(NY, NZH, NX, NZL, ROWS, BS),
            stats[0],
            roots.reshape(NX * NZL, NC, ROWS, BS),
            refresh,
        )
    )
    hbm = pl.BlockSpec(memory_space=pltpu.HBM)
    vmem = pl.BlockSpec(memory_space=pltpu.VMEM)
    everything = (NZH, NX, NZL, ROWS, BS)
    pieces = (CHUNKS, WIDE, ROWS, BS)
    whole = (NX * NZL, NC, ROWS, BS)
    square = (BS, BS)
    dma = pltpu.SemaphoreType.DMA
    outs = ((square, F32), (square, BF), ((NX * NZL, ROWS, BS), BF))
    done = pl.pallas_call(
        kernel,
        out_shape=tuple(pltpu.VMEM(shape, kind) for shape, kind in outs),
        in_specs=[hbm] * 4,
        out_specs=(vmem,) * 3,
        scratch_shapes=[
            *[pltpu.VMEM(everything, BF) for _ in range(3)],
            *[pltpu.VMEM(pieces, BF) for _ in range(6)],
            pltpu.VMEM((NZH, NZL, NX, ROWS, BS), BF),
            pltpu.VMEM((NX, NZL, NC, ROWS, BS), BF),
            pltpu.VMEM(square, F32),
            pltpu.VMEM(whole, BF),
            pltpu.VMEM(whole, BF),
            pltpu.VMEM(square, F32),
            pltpu.VMEM(square, BF),
            pltpu.VMEM(square, F32),
            pltpu.VMEM(square, BF),
            pltpu.VMEM(square, F32),
            pltpu.VMEM(square, BF),
            pltpu.VMEM(square, BF),
            pltpu.VMEM((BS // NC, BS), BF),
            pltpu.VMEM((NX * NZL, ROWS, BS), BF),
            pltpu.SMEM((NX * NZL,), jnp.int32),
            dma((6,)),
            dma((3, 2, CHUNKS)),
            dma((3, 2, CHUNKS)),
            dma((2, CHUNKS, WIDE)),
            dma((NZH, NZL, NX)),
            dma((NZL + 1,)),
            dma((NZL + 1,)),
            dma((NX * NZL,)),
            dma((NX * NZL,)),
            pltpu.SemaphoreType.REGULAR((5,)),
        ],
        compiler_params=pltpu.CompilerParams(
            collective_id=0, has_side_effects=True, vmem_limit_bytes=40 * 1024 * 1024
        ),
        name="shampoo",
    )(*here)
    new_stats, new_roots, update = pl.pallas_call(
        write_out,
        out_shape=tuple(pltpu.HBM(shape, kind) for shape, kind in outs),
        in_specs=[vmem] * 3,
        out_specs=(hbm,) * 3,
        scratch_shapes=[dma((3,))],
        name="write_out",
    )(*(pltpu.with_memory_space_constraint(value, pltpu.VMEM) for value in done))
    return new_stats[None], new_roots[None], update


def solution(mesh):
    placed = (
        P("dp", None, "owner", None),
        P(("dp", "owner"), None, None),
        P(("dp", "owner"), None, None),
        P("dp"),
    )
    return jax.shard_map(
        local,
        mesh=mesh,
        in_specs=placed,
        out_specs=(
            P(("dp", "owner"), None, None),
            P(("dp", "owner"), None, None),
            P("dp", "owner", None),
        ),
        check_vma=False,
    )
```
